32 devices in a mesh: kq: 16 (over z, y, x), band: 2 (over core).
Axes of the slice: x: 2, y: 2, z: 4, core: 2. Of those that a mesh axis runs over, the one named last changes fastest.
Arguments:
- orbitals: bfloat16 [16, 16, 4096], P('kq', 'band'), may hold values from -6 to 6
- screening: bfloat16 [32, 1024, 1024], P('kq'), may hold values from -0.1875 to 0.1875
- pair_k: int32 [32, 2], replicated, may hold values from 0 to 15, as said below
- pair_q: int32 [32], P('kq'), may hold values from 0 to 31, as said below
- gmap: int32 [1024], replicated, may hold values from 0 to 4095, as said below
Outputs:
- exch_field: float32 [16, 16, 4096], P('kq', 'band')
The draws below stay inside these ranges and needn't reach their ends.
Inputs may be any that keep to these rules, and one draw needn't show every extreme that they name: Rows are grouped by owner: rows o * 2 to (o + 1) * 2 - 1 belong to kq index o, and pair_k[o * 2 + i, s] = (pair_k[i, s] + o) mod 16 for every row i of owner 0 and both columns s. The 2 * 2 k-points of one owner are all different, and those of owner 0 include 16 - 1 and 8. `pair_q`: row i names one of the 2 transfers of owner o = i // 2, namely 2 * o to 2 * o + 1, and each of them in 1 of the owner's rows. `gmap`: all entries differ; 0 and 4095 are among them.
All inputs are finite; a program needn't handle non-finite values.
Results may differ from the reference program's by a relative error of at most 0.007.
Values may be sent and summed in bfloat16 or wider, within the bound.
No kernel may reach another device: no remote copies, remote signals or barrier semaphores. Data moves between devices by JAX's collectives and lax.ppermute only.
A program may use at most 128 MiB of HBM per device.

```python
import math
import jax
import jax.numpy as jnp
from jax import lax

GRID = 16
R = 4096
NG = 1024
NB = 16
Q_DEV = 2
P_DEV = 2
NK = 16
NQ = 32
PAIRS = 32


def draw_pair_k(key, part):
    rest = jax.random.permutation(jax.random.fold_in(key, 11), NK - 2)[:2 * P_DEV - 2].astype(jnp.int32)
    rest = rest + (rest >= NK // 2).astype(jnp.int32)
    fixed_pair = jnp.array([NK - 1, NK // 2], jnp.int32)
    listed = jnp.concatenate([fixed_pair, rest])
    order = jax.random.permutation(jax.random.fold_in(key, 13), 2 * P_DEV)
    offsets = listed[order].astype(jnp.int32)
    owners = jnp.arange(NK, dtype=jnp.int32)
    refs = (owners[:, None] + offsets[None, :]) % NK
    first_points = refs[:, :P_DEV].reshape(PAIRS)
    second_points = refs[:, P_DEV:].reshape(PAIRS)
    return jnp.stack([first_points, second_points], axis=1).astype(jnp.int32)


def draw_pair_q(key, part):
    shifts = jax.random.randint(jax.random.fold_in(key, 23), (NK, 1), 0, Q_DEV).astype(jnp.int32)
    owners = jnp.arange(NK, dtype=jnp.int32)[:, None]
    within = jnp.arange(P_DEV, dtype=jnp.int32)[None, :]
    return (owners * Q_DEV + (within + shifts) % Q_DEV).reshape(PAIRS).astype(jnp.int32)


def draw_gmap(key, part):
    inner = jax.random.permutation(jax.random.fold_in(key, 31), GRID ** 3 - 2)[:NG - 2].astype(jnp.int32) + 1
    listed = jnp.concatenate([jnp.array([0, GRID ** 3 - 1], jnp.int32), inner])
    order = jax.random.permutation(jax.random.fold_in(key, 37), NG)
    return listed[order].astype(jnp.int32)


def level_of(own_key, extent, cuts, least, largest):
    level, own = 1.0, jax.random.fold_in(own_key, 6)
    for position, shards_of in cuts:
        draws = jnp.exp(jax.random.uniform(jax.random.fold_in(own, position), (shards_of,), jnp.float32, least / len(cuts), largest / len(cuts)))
        level = level * jnp.repeat(draws, extent[position] // shards_of).reshape([-1 if axis == position else 1 for axis in range(len(extent))])
    return level


def noise(rng, shape, spread, most, split=(), held_as=jnp.bfloat16):
    values = spread * jax.random.normal(rng, shape, jnp.float32)
    if split:
        values = values * level_of(rng, shape, split, -0.22, 0.18)
    return jnp.clip(values, -most, most).astype(held_as)


def setup_inputs(seed: int = 0) -> dict:
    key_list = jax.random.split(jax.random.key(seed), 6)
    orbitals = noise(key_list[0], (NK, NB, R), 1.0, 6.0, ((0, 16), (1, 2)))
    screening = noise(key_list[1], (NQ, NG, NG), NG ** -0.5, 0.1875, ((0, 16),))
    pair_k = draw_pair_k(jax.random.fold_in(key_list[5], 71), 0)
    pair_q = draw_pair_q(jax.random.fold_in(key_list[5], 71), 0)
    gmap = draw_gmap(jax.random.fold_in(key_list[5], 71), 0)
    return dict(orbitals=orbitals, screening=screening, pair_k=pair_k, pair_q=pair_q, gmap=gmap)


def cas_table(gmap, grid_side):
    cells = grid_side ** 3
    points = jnp.arange(cells, dtype=jnp.int32)
    coord_x = points // (grid_side * grid_side)
    coord_y = points // grid_side % grid_side
    coord_z = points % grid_side
    freq_x = gmap // (grid_side * grid_side)
    freq_y = gmap // grid_side % grid_side
    freq_z = gmap % grid_side
    phase = (freq_x[:, None] * coord_x[None, :] + freq_y[:, None] * coord_y[None, :] + freq_z[:, None] * coord_z[None, :]) % grid_side
    angle = phase.astype(jnp.float32) * (2.0 * math.pi / grid_side)
    return (jnp.cos(angle) + jnp.sin(angle)).astype(jnp.bfloat16)

def pair_fields(left_block, right_block, screen_mat, table):
    rows_left = left_block.shape[0]
    rows_right = right_block.shape[0]
    cells = table.shape[1]
    factor = 1.0 / math.sqrt(cells)
    density = (left_block.astype(jnp.float32)[:, None, :] * right_block.astype(jnp.float32)[None, :, :]).astype(jnp.bfloat16)
    density = density.reshape(rows_left * rows_right, cells)
    table32 = table.astype(jnp.float32)
    spectrum = (jnp.dot(density.astype(jnp.float32), table32.T, preferred_element_type=jnp.float32) * factor).astype(jnp.bfloat16)
    screened = jnp.dot(spectrum.astype(jnp.float32), screen_mat.astype(jnp.float32), preferred_element_type=jnp.float32).astype(jnp.bfloat16)
    potential = (jnp.dot(screened.astype(jnp.float32), table32, preferred_element_type=jnp.float32) * factor).astype(jnp.bfloat16)
    potential = potential.reshape(rows_left, rows_right, cells).astype(jnp.float32)
    toward_left = jnp.einsum('mnr,nr->mr', potential, right_block.astype(jnp.float32))
    toward_right = jnp.einsum('mnr,mr->nr', potential, left_block.astype(jnp.float32))
    return (toward_left, toward_right)

def reference(orbitals, screening, pair_k, pair_q, gmap):
    table = cas_table(gmap, GRID)

    def accumulate(index, totals):
        first_point = pair_k[index, 0]
        second_point = pair_k[index, 1]
        transfer = pair_q[index]
        left_block = lax.dynamic_index_in_dim(orbitals, first_point, 0, keepdims=False)
        right_block = lax.dynamic_index_in_dim(orbitals, second_point, 0, keepdims=False)
        screen_mat = lax.dynamic_index_in_dim(screening, transfer, 0, keepdims=False)
        toward_left, toward_right = pair_fields(left_block, right_block, screen_mat, table)
        totals = totals.at[first_point].add(toward_left)
        totals = totals.at[second_point].add(toward_right)
        return totals
    zeros_init = jnp.zeros(orbitals.shape, jnp.float32)
    return lax.fori_loop(0, PAIRS, accumulate, zeros_init)
```

```python
import functools
import math

import jax
import jax.numpy as jnp
from jax import lax
from jax.experimental import pallas as pl
from jax.experimental.pallas import tpu as pltpu
from jax.sharding import PartitionSpec as P

MOST_BRANCHES = 256
F32 = jnp.float32
BF16 = jnp.bfloat16
TILE = 256


def circle(freq, side):
    steps = lax.broadcasted_iota(jnp.int32, (side, freq.shape[1]), 0)
    angle = lax.rem(steps * freq, side).astype(F32) * (2.0 * math.pi / side)
    return jnp.cos(angle), jnp.sin(angle)


def fill_table(gmap, table, plane, mirror, side):
    face = side * side
    cos_x, sin_x = circle(gmap // face, side)
    cos_y, sin_y = circle(lax.rem(gmap // side, side), side)
    cos_z, sin_z = circle(lax.rem(gmap, side), side)
    cas_z, anti_z = cos_z + sin_z, cos_z - sin_z
    for y in range(side):
        rows = slice(y * side, (y + 1) * side)
        plane[rows, :] = cos_y[y : y + 1] * cas_z + sin_y[y : y + 1] * anti_z
        mirror[rows, :] = cos_y[y : y + 1] * anti_z - sin_y[y : y + 1] * cas_z
    for x in range(side):
        table[x * face : (x + 1) * face, :] = (
            cos_x[x : x + 1] * plane[...] + sin_x[x : x + 1] * mirror[...]
        ).astype(BF16)


def pair_kernel(
    side, own_q, q_ref, gmap_ref, left, right, screening, to_left, to_right,
    table, plane, mirror, density, spectrum, screened, matrix, arrival,
):
    slot = q_ref[lax.axis_index("band")] - lax.axis_index("kq") * own_q
    fetch = pltpu.make_async_copy(screening.at[slot], matrix, arrival)
    fetch.start()
    rows_left, cells = left.shape
    rows_right = right.shape[0]
    waves = table.shape[1]
    factor = 1.0 / math.sqrt(cells)
    fill_table(gmap_ref[...], table, plane, mirror, side)
    for m in range(rows_left):
        density[m * rows_right : (m + 1) * rows_right, :] = (
            left[m : m + 1, :].astype(F32) * right[...].astype(F32)
        ).astype(BF16)
    for start in range(0, waves, TILE):
        part = slice(start, start + TILE)
        total = jnp.dot(density[...], table[:, part], preferred_element_type=F32)
        spectrum[:, part] = (total * factor).astype(BF16)
    fetch.wait()
    screened[...] = jnp.dot(
        spectrum[...], matrix[...], preferred_element_type=F32
    ).astype(BF16)
    for start in range(0, cells, TILE):
        part = slice(start, start + TILE)
        potential = lax.dot_general(
            screened[...], table[part, :], (((1,), (1,)), ((), ())), preferred_element_type=F32
        )
        potential = potential.reshape(rows_left, rows_right, TILE)
        left32, right32 = left[:, part].astype(F32), right[:, part].astype(F32)
        to_left[:, part] = (jnp.sum(potential * right32[None], axis=1) * factor).astype(BF16)
        to_right[:, part] = (jnp.sum(potential * left32[:, None], axis=0) * factor).astype(BF16)


def pair_fields(left, right, screening, pair_q, gmap):
    rows_left, cells = left.shape
    rows_right = right.shape[0]
    waves = gmap.shape[0]
    side = round(cells ** (1 / 3))
    vmem = pl.BlockSpec(memory_space=pltpu.VMEM)
    return pl.pallas_call(
        functools.partial(pair_kernel, side, screening.shape[0]),
        out_shape=(
            jax.ShapeDtypeStruct((rows_left, cells), BF16),
            jax.ShapeDtypeStruct((rows_right, cells), BF16),
        ),
        in_specs=[
            pl.BlockSpec(memory_space=pltpu.SMEM), vmem, vmem, vmem, pl.BlockSpec(memory_space=pl.ANY),
        ],
        out_specs=(vmem, vmem),
        scratch_shapes=[
            pltpu.VMEM((cells, waves), BF16),
            pltpu.VMEM((side * side, waves), F32),
            pltpu.VMEM((side * side, waves), F32),
            pltpu.VMEM((rows_left * rows_right, cells), BF16),
            pltpu.VMEM((rows_left * rows_right, waves), BF16),
            pltpu.VMEM((rows_left * rows_right, waves), BF16),
            pltpu.VMEM((waves, waves), BF16),
            pltpu.SemaphoreType.DMA,
        ],
        compiler_params=pltpu.CompilerParams(vmem_limit_bytes=28 * 2**20),
    )(pair_q, gmap.reshape(1, waves), left, right, screening)


def shifted(value, shift, count):
    return lax.ppermute(value, "kq", [(i, (i + shift) % count) for i in range(count)])


def move(first, second, low, high, count, sign):
    pairs = [(i, j) for i in range(count) for j in range(i + 1, count)]
    if len(pairs) <= MOST_BRANCHES:
        chosen = low * (2 * count - 1 - low) // 2 + high - low - 1
        moves = [
            lambda a, b, i=i, j=j: (shifted(a, sign * i, count), shifted(b, sign * j, count))
            for i, j in pairs
        ]
        return lax.switch(chosen, moves, first, second)
    moves = [lambda a, i=i: shifted(a, sign * i, count) for i in range(count)]
    return lax.switch(low, moves, first), lax.switch(high, moves, second)


def shards(orbitals, screening, pair_k, pair_q, gmap):
    count = lax.axis_size("kq")
    bands = lax.axis_size("band")
    core = lax.axis_index("band")
    rows = orbitals.shape[1]
    offsets = lax.dynamic_index_in_dim(pair_k, core, 0, keepdims=False)
    low, high = jnp.min(offsets), jnp.max(offsets)
    block = lax.all_gather(orbitals[0], "band", axis=0, tiled=True)
    left, right = move(block, block, low, high, count, -1)
    to_left, to_right = pair_fields(left, right, screening, pair_q, gmap)
    to_left, to_right = move(to_left, to_right, low, high, count, 1)
    total = to_left.astype(F32) + to_right.astype(F32)
    theirs = lax.dynamic_slice_in_dim(total, (1 - core) * rows, rows, 0).astype(BF16)
    mine = lax.dynamic_slice_in_dim(total, core * rows, rows, 0)
    other = lax.ppermute(theirs, "band", [(i, (i + 1) % bands) for i in range(bands)])
    return (mine + other.astype(F32))[None]


def solution(mesh):
    in_specs = (P("kq", "band", None), P("kq", None, None), P(), P("kq"), P())
    out_specs = P("kq", "band", None)
    return jax.shard_map(shards, mesh=mesh, in_specs=in_specs, out_specs=out_specs, check_vma=False)
```

```python
import functools
import math

import jax
import jax.numpy as jnp
from jax import lax
from jax.experimental import pallas as pl
from jax.experimental.pallas import tpu as pltpu
from jax.sharding import PartitionSpec as P

F32 = jnp.float32
BF16 = jnp.bfloat16
TILE = 256


def circle(freq, side):
    steps = lax.broadcasted_iota(jnp.int32, (side, freq.shape[1]), 0)
    angle = lax.rem(steps * freq, side).astype(F32) * (2.0 * math.pi / side)
    return jnp.cos(angle), jnp.sin(angle)


def fill_planes(gmap, cos_x, sin_x, plane, mirror, side):
    face = side * side
    cos_x[...], sin_x[...] = circle(gmap // face, side)
    cos_y, sin_y = circle(lax.rem(gmap // side, side), side)
    cos_z, sin_z = circle(lax.rem(gmap, side), side)
    cas_z, anti_z = cos_z + sin_z, cos_z - sin_z
    for y in range(side):
        rows = slice(y * side, (y + 1) * side)
        plane[rows, :] = cos_y[y : y + 1] * cas_z + sin_y[y : y + 1] * anti_z
        mirror[rows, :] = cos_y[y : y + 1] * anti_z - sin_y[y : y + 1] * cas_z


def fill_table(table, cos_x, sin_x, plane, mirror, side, part):
    face, half = side * side, side // 2
    turn = cos_x[half : half + 1, part].astype(BF16)
    along, against = plane[:, part], mirror[:, part]

    def put(x, value):
        value = value.astype(BF16)
        table[x * face : (x + 1) * face, part] = value
        other = (x + half) % side
        table[other * face : (other + 1) * face, part] = value * turn

    put(0, along)
    put(half // 2, cos_x[half // 2 : half // 2 + 1, part] * along + sin_x[half // 2 : half // 2 + 1, part] * against)
    for x in range(1, half // 2):
        even = cos_x[x : x + 1, part] * along
        odd = sin_x[x : x + 1, part] * against
        put(x, even + odd)
        put(side - x, even - odd)


def pair_kernel(
    side, slot_far, gmap_far, left_far, right_far, screening, to_left, to_right,
    slot, gmap, left, right, matrix, cos_x, sin_x, plane, mirror, table, density, spectrum, screened, arrival,
):
    def fetch(i, source, target):
        copy = pltpu.make_async_copy(source, target, arrival.at[i])
        copy.start()
        return copy

    get_gmap = fetch(0, gmap_far, gmap)
    get_slot = fetch(1, slot_far, slot)
    get_left = fetch(2, left_far, left)
    get_right = fetch(3, right_far, right)
    get_slot.wait()
    own = slot[0] - lax.axis_index("kq") * screening.shape[0]
    get_matrix = fetch(4, screening.at[own], matrix)

    rows_left, cells = left.shape
    rows_right = right.shape[0]
    waves = table.shape[1]
    factor = 1.0 / math.sqrt(cells)
    parts = [slice(start, start + TILE) for start in range(0, waves, TILE)]
    get_gmap.wait()
    fill_planes(gmap[...], cos_x, sin_x, plane, mirror, side)
    fill_table(table, cos_x, sin_x, plane, mirror, side, parts[0])
    get_left.wait()
    get_right.wait()
    for m in range(rows_left):
        density[m * rows_right : (m + 1) * rows_right, :] = (
            left[m : m + 1, :].astype(F32) * right[...].astype(F32)
        ).astype(BF16)
    for i, part in enumerate(parts):
        total = jnp.dot(density[...], table[:, part], preferred_element_type=F32)
        if i + 1 < len(parts):
            fill_table(table, cos_x, sin_x, plane, mirror, side, parts[i + 1])
        spectrum[:, part] = (total * factor).astype(BF16)
    get_matrix.wait()
    screened[...] = jnp.dot(
        spectrum[...], matrix[...], preferred_element_type=F32
    ).astype(BF16)
    for start in range(0, cells, TILE):
        part = slice(start, start + TILE)
        potential = lax.dot_general(
            screened[...], table[part, :], (((1,), (1,)), ((), ())), preferred_element_type=F32
        )
        potential = potential.reshape(rows_left, rows_right, TILE)
        left32, right32 = left[:, part].astype(F32), right[:, part].astype(F32)
        to_left[:, part] = (jnp.sum(potential * right32[None], axis=1) * factor).astype(BF16)
        to_right[:, part] = (jnp.sum(potential * left32[:, None], axis=0) * factor).astype(BF16)


def pair_fields(left, right, screening, slot, gmap):
    rows_left, cells = left.shape
    rows_right = right.shape[0]
    waves = gmap.shape[0]
    side = round(cells ** (1 / 3))
    vmem = pl.BlockSpec(memory_space=pltpu.VMEM)
    far = pl.BlockSpec(memory_space=pltpu.HBM)
    return pl.pallas_call(
        functools.partial(pair_kernel, side),
        out_shape=(
            jax.ShapeDtypeStruct((rows_left, cells), BF16),
            jax.ShapeDtypeStruct((rows_right, cells), BF16),
        ),
        in_specs=[far] * 5,
        out_specs=(vmem, vmem),
        scratch_shapes=[
            pltpu.SMEM((1,), jnp.int32),
            pltpu.VMEM((1, waves), jnp.int32),
            pltpu.VMEM((rows_left, cells), BF16),
            pltpu.VMEM((rows_right, cells), BF16),
            pltpu.VMEM((waves, waves), BF16),
            pltpu.VMEM((side, waves), F32),
            pltpu.VMEM((side, waves), F32),
            pltpu.VMEM((side * side, waves), F32),
            pltpu.VMEM((side * side, waves), F32),
            pltpu.VMEM((cells, waves), BF16),
            pltpu.VMEM((rows_left * rows_right, cells), BF16),
            pltpu.VMEM((rows_left * rows_right, waves), BF16),
            pltpu.VMEM((rows_left * rows_right, waves), BF16),
            pltpu.SemaphoreType.DMA((5,)),
        ],
        compiler_params=pltpu.CompilerParams(vmem_limit_bytes=60 * 2**20),
    )(slot, gmap.reshape(1, waves), left, right, screening)


def fixed_shift(value, count, sign):
    shifts = (count - 1, count // 2)
    route = [
        (2 * i + core, 2 * ((i + sign * shift) % count) + core)
        for i in range(count)
        for core, shift in enumerate(shifts)
    ]
    return lax.ppermute(value, ("kq", "band"), route)


def chosen_shift(value, steps, count, sign):
    moves = [
        lambda a, i=i: lax.ppermute(a, "kq", [(j, (j + sign * i) % count) for j in range(count)])
        for i in range(count)
    ]
    return lax.switch(steps, moves, value)


def cross(value):
    return lax.ppermute(value, "band", [(0, 1), (1, 0)])


def plan(pair_k, pair_q, core, count):
    last, half = count - 1, count // 2
    own = jnp.where(core == 0, last, half)
    other = last + half - own
    left, right = pair_k[: pair_q.shape[0], 0], pair_k[: pair_q.shape[0], 1]
    left_fixed, right_fixed = (left == last) | (left == half), (right == last) | (right == half)
    take_left = ((right == own) & (left != other)) | ~(left_fixed | right_fixed | (core != 0))
    take_right = ((left == own) & (right != other)) | ~(left_fixed | right_fixed | (core == 0))
    steps = jnp.sum(jnp.where(take_left, left, 0) + jnp.where(take_right, right, 0))
    together = jnp.sum((left_fixed & right_fixed).astype(jnp.int32))
    mine = ((left == last) | (right == last)) == (core == 0)
    slot = jnp.sum(jnp.where(mine, pair_q, 0))
    return steps, together, slot.reshape(1)


def shards(orbitals, screening, pair_k, pair_q, gmap):
    count = lax.axis_size("kq")
    core = lax.axis_index("band")
    rows = orbitals.shape[1]
    first = core == 0
    steps, together, slot = plan(pair_k, pair_q, core, count)

    def bring_apart(block):
        return fixed_shift(block, count, -1), chosen_shift(block, steps, count, -1)

    def bring_together(block):
        fixed, chosen = bring_apart(block)
        return jnp.where(first, fixed, chosen), cross(jnp.where(first, chosen, fixed))

    def return_apart(fixed, chosen):
        fixed = fixed_shift(fixed, count, 1)
        return fixed, chosen_shift(chosen, steps, count, 1)

    def return_together(kept, lent):
        lent = cross(lent)
        return return_apart(jnp.where(first, kept, lent), jnp.where(first, lent, kept))

    block = lax.all_gather(orbitals[0], "band", axis=0, tiled=True)
    left, right = lax.switch(together, [bring_apart, bring_together], block)
    to_left, to_right = pair_fields(left, right, screening, slot, gmap)
    to_left, to_right = lax.switch(together, [return_apart, return_together], to_left, to_right)
    total = to_left.astype(F32) + to_right.astype(F32)
    theirs = lax.dynamic_slice_in_dim(total, (1 - core) * rows, rows, 0).astype(BF16)
    mine = lax.dynamic_slice_in_dim(total, core * rows, rows, 0)
    return (mine + cross(theirs).astype(F32))[None]


def solution(mesh):
    in_specs = (P("kq", "band", None), P("kq", None, None), P(), P("kq"), P())
    out_specs = P("kq", "band", None)
    return jax.shard_map(shards, mesh=mesh, in_specs=in_specs, out_specs=out_specs, check_vma=False)
```

```python
import functools
import math

import jax
import jax.numpy as jnp
from jax import lax
from jax.experimental import pallas as pl
from jax.experimental.pallas import tpu as pltpu
from jax.sharding import PartitionSpec as P

F32 = jnp.float32
BF16 = jnp.bfloat16
TILE = 256


def circle(freq, side):
    steps = lax.broadcasted_iota(jnp.int32, (side, freq.shape[1]), 0)
    angle = lax.rem(steps * freq, side).astype(F32) * (2.0 * math.pi / side)
    return jnp.cos(angle), jnp.sin(angle)


def fill_planes(gmap, cos_x, sin_x, plane, mirror, side):
    face = side * side
    cos_x[...], sin_x[...] = circle(gmap // face, side)
    cos_y, sin_y = circle(lax.rem(gmap // side, side), side)
    cos_z, sin_z = circle(lax.rem(gmap, side), side)
    cas_z, anti_z = cos_z + sin_z, cos_z - sin_z
    for y in range(side):
        rows = slice(y * side, (y + 1) * side)
        plane[rows, :] = cos_y[y : y + 1] * cas_z + sin_y[y : y + 1] * anti_z
        mirror[rows, :] = cos_y[y : y + 1] * anti_z - sin_y[y : y + 1] * cas_z


def fill_table(table, cos_x, sin_x, plane, mirror, side, part):
    face, half = side * side, side // 2
    turn = cos_x[half : half + 1, part].astype(BF16)
    along, against = plane[:, part], mirror[:, part]

    def put(x, value):
        value = value.astype(BF16)
        table[x * face : (x + 1) * face, part] = value
        other = (x + half) % side
        table[other * face : (other + 1) * face, part] = value * turn

    put(0, along)
    put(half // 2, cos_x[half // 2 : half // 2 + 1, part] * along + sin_x[half // 2 : half // 2 + 1, part] * against)
    for x in range(1, half // 2):
        even = cos_x[x : x + 1, part] * along
        odd = sin_x[x : x + 1, part] * against
        put(x, even + odd)
        put(side - x, even - odd)


def pair_kernel(
    side, slot, gmap, left, right, screening, to_left, to_right,
    matrix, cos_x, sin_x, plane, mirror, table, density, spectrum, screened, arrival,
):
    def fetch(i, source, target):
        copy = pltpu.make_async_copy(source, target, arrival.at[i])
        copy.start()
        return copy

    own = slot[0] - lax.axis_index("kq") * screening.shape[0]
    get_matrix = fetch(2, screening.at[own], matrix)

    rows_left, cells = left.shape
    rows_right = right.shape[0]
    waves = table.shape[1]
    factor = 1.0 / math.sqrt(cells)
    parts = [slice(start, start + TILE) for start in range(0, waves, TILE)]
    fill_planes(gmap[...], cos_x, sin_x, plane, mirror, side)
    fill_table(table, cos_x, sin_x, plane, mirror, side, parts[0])
    for m in range(rows_left):
        density[m * rows_right : (m + 1) * rows_right, :] = (
            left[m : m + 1, :].astype(F32) * right[...].astype(F32)
        ).astype(BF16)
    for i, part in enumerate(parts):
        total = jnp.dot(density[...], table[:, part], preferred_element_type=F32)
        if i + 1 < len(parts):
            fill_table(table, cos_x, sin_x, plane, mirror, side, parts[i + 1])
        spectrum[:, part] = (total * factor).astype(BF16)
    get_matrix.wait()
    screened[...] = jnp.dot(
        spectrum[...], matrix[...], preferred_element_type=F32
    ).astype(BF16)
    for start in range(0, cells, TILE):
        part = slice(start, start + TILE)
        potential = lax.dot_general(
            screened[...], table[part, :], (((1,), (1,)), ((), ())), preferred_element_type=F32
        )
        potential = potential.reshape(rows_left, rows_right, TILE)
        left32, right32 = left[:, part].astype(F32), right[:, part].astype(F32)
        to_left[:, part] = (jnp.sum(potential * right32[None], axis=1) * factor).astype(BF16)
        to_right[:, part] = (jnp.sum(potential * left32[:, None], axis=0) * factor).astype(BF16)


def pair_fields(left, right, screening, slot, gmap):
    rows_left, cells = left.shape
    rows_right = right.shape[0]
    waves = gmap.shape[0]
    side = round(cells ** (1 / 3))
    vmem = pl.BlockSpec(memory_space=pltpu.VMEM)
    far = pl.BlockSpec(memory_space=pltpu.HBM)
    return pl.pallas_call(
        functools.partial(pair_kernel, side),
        out_shape=(
            jax.ShapeDtypeStruct((rows_left, cells), BF16),
            jax.ShapeDtypeStruct((rows_right, cells), BF16),
        ),
        in_specs=[pl.BlockSpec(memory_space=pltpu.SMEM), vmem, vmem, vmem, far],
        out_specs=(vmem, vmem),
        scratch_shapes=[
            pltpu.VMEM((waves, waves), BF16),
            pltpu.VMEM((side, waves), F32),
            pltpu.VMEM((side, waves), F32),
            pltpu.VMEM((side * side, waves), F32),
            pltpu.VMEM((side * side, waves), F32),
            pltpu.VMEM((cells, waves), BF16),
            pltpu.VMEM((rows_left * rows_right, cells), BF16),
            pltpu.VMEM((rows_left * rows_right, waves), BF16),
            pltpu.VMEM((rows_left * rows_right, waves), BF16),
            pltpu.SemaphoreType.DMA((3,)),
        ],
        compiler_params=pltpu.CompilerParams(vmem_limit_bytes=60 * 2**20),
    )(slot, gmap.reshape(1, waves), left, right, screening)


def fixed_shift(value, count, sign):
    shifts = (count - 1, count // 2)
    route = [
        (2 * i + core, 2 * ((i + sign * shift) % count) + core)
        for i in range(count)
        for core, shift in enumerate(shifts)
    ]
    return lax.ppermute(value, ("kq", "band"), route)


def chosen_shift(value, steps, count, sign):
    moves = [
        lambda a, i=i: lax.ppermute(a, "kq", [(j, (j + sign * i) % count) for j in range(count)])
        for i in range(count)
    ]
    return lax.switch(steps, moves, value)


def cross(value):
    return lax.ppermute(value, "band", [(0, 1), (1, 0)])


def plan(pair_k, pair_q, core, count):
    last, half = count - 1, count // 2
    own = jnp.where(core == 0, last, half)
    other = last + half - own
    left, right = pair_k[: pair_q.shape[0], 0], pair_k[: pair_q.shape[0], 1]
    left_fixed, right_fixed = (left == last) | (left == half), (right == last) | (right == half)
    take_left = ((right == own) & (left != other)) | ~(left_fixed | right_fixed | (core != 0))
    take_right = ((left == own) & (right != other)) | ~(left_fixed | right_fixed | (core == 0))
    steps = jnp.sum(jnp.where(take_left, left, 0) + jnp.where(take_right, right, 0))
    together = jnp.sum((left_fixed & right_fixed).astype(jnp.int32))
    mine = ((left == last) | (right == last)) == (core == 0)
    slot = jnp.sum(jnp.where(mine, pair_q, 0))
    return steps, together, slot


def shards(orbitals, screening, pair_k, pair_q, gmap):
    count = lax.axis_size("kq")
    core = lax.axis_index("band")
    rows = orbitals.shape[1]
    first = core == 0
    steps, together, slot = plan(pair_k, pair_q, core, count)

    def lend(fixed, chosen):
        return jnp.where(first, fixed, chosen), cross(jnp.where(first, chosen, fixed))

    def regain(kept, lent):
        lent = cross(lent)
        return jnp.where(first, kept, lent), jnp.where(first, lent, kept)

    block = jnp.concatenate([orbitals[0], cross(orbitals[0])])
    block, steps, together, slot = lax.optimization_barrier((block, steps, together, slot))
    fixed = fixed_shift(block, count, -1)
    chosen = chosen_shift(block, steps, count, -1)
    kept, given = lax.switch(together, [lambda a, b: (a, b), lend], fixed, chosen)
    kept, given = pair_fields(kept, given, screening, slot.reshape(1), gmap)
    fixed, chosen = lax.switch(together, [lambda a, b: (a, b), regain], kept, given)
    fixed = fixed_shift(fixed, count, 1)
    chosen = chosen_shift(chosen, steps, count, 1)
    total = fixed.astype(F32) + chosen.astype(F32)
    return (total[:rows] + cross(total[rows:].astype(BF16)).astype(F32))[None]


def solution(mesh):
    in_specs = (P("kq", "band", None), P("kq", None, None), P(), P("kq"), P())
    out_specs = P("kq", "band", None)
    return jax.shard_map(shards, mesh=mesh, in_specs=in_specs, out_specs=out_specs, check_vma=False)
```

```python
import functools
import math

import jax
import jax.numpy as jnp
from jax import lax
from jax.experimental import pallas as pl
from jax.experimental.pallas import tpu as pltpu
from jax.sharding import PartitionSpec as P

F32 = jnp.float32
BF16 = jnp.bfloat16
TILE = 256


def cosine(phase, side):
    phase = jnp.minimum(phase, side - phase)
    beyond = 4 * phase > side
    angle = jnp.where(beyond, side // 2 - phase, phase).astype(F32) * (2.0 * math.pi / side)
    square = angle * angle
    value = jnp.full(phase.shape, 1.0 / math.factorial(12), F32)
    for order in range(10, -1, -2):
        value = value * square + (-1.0) ** (order // 2) / math.factorial(order)
    return jnp.where(beyond, -value, value)


def circle(freq, side):
    steps = lax.broadcasted_iota(jnp.int32, (side, freq.shape[1]), 0)
    phase = lax.rem(steps * freq, side)
    return cosine(phase, side), cosine(lax.rem(phase + (side - side // 4), side), side)


def fill_table(gmap, table, plane, mirror, side, part):
    face, half = side * side, side // 2
    freq = gmap[:, part]
    cos_x, sin_x = circle(freq // face, side)
    cos_y, sin_y = circle(lax.rem(freq // side, side), side)
    cos_z, sin_z = circle(lax.rem(freq, side), side)
    cas_z, anti_z = cos_z + sin_z, cos_z - sin_z
    for y in range(side):
        rows = slice(y * side, (y + 1) * side)
        plane[rows, part] = cos_y[y : y + 1] * cas_z + sin_y[y : y + 1] * anti_z
        mirror[rows, part] = cos_y[y : y + 1] * anti_z - sin_y[y : y + 1] * cas_z
    turn = cos_x[half : half + 1].astype(BF16)
    along, against = plane[:, part], mirror[:, part]

    def put(x, value):
        value = value.astype(BF16)
        table[x * face : (x + 1) * face, part] = value
        other = (x + half) % side
        table[other * face : (other + 1) * face, part] = value * turn

    put(0, along)
    quarter = half // 2
    put(quarter, cos_x[quarter : quarter + 1] * along + sin_x[quarter : quarter + 1] * against)
    for x in range(1, quarter):
        even = cos_x[x : x + 1] * along
        odd = sin_x[x : x + 1] * against
        put(x, even + odd)
        put(side - x, even - odd)


def pair_kernel(
    side, slot, gmap, left, right, screening, to_left, to_right,
    matrix, plane, mirror, table, density, spectrum, screened, arrival,
):
    def fetch(i, source, target):
        copy = pltpu.make_async_copy(source, target, arrival.at[i])
        copy.start()
        return copy

    own = slot[0] - lax.axis_index("kq") * screening.shape[0]
    get_matrix = fetch(2, screening.at[own], matrix)

    rows_left, cells = left.shape
    rows_right = right.shape[0]
    waves = table.shape[1]
    factor = 1.0 / math.sqrt(cells)
    parts = [slice(start, start + TILE) for start in range(0, waves, TILE)]
    fill_table(gmap, table, plane, mirror, side, parts[0])
    for m in range(rows_left):
        density[m * rows_right : (m + 1) * rows_right, :] = (
            left[m : m + 1, :].astype(F32) * right[...].astype(F32)
        ).astype(BF16)
    for i, part in enumerate(parts):
        total = jnp.dot(density[...], table[:, part], preferred_element_type=F32)
        if i + 1 < len(parts):
            fill_table(gmap, table, plane, mirror, side, parts[i + 1])
        spectrum[:, part] = (total * factor).astype(BF16)
    get_matrix.wait()
    screened[...] = jnp.dot(
        spectrum[...], matrix[...], preferred_element_type=F32
    ).astype(BF16)
    for start in range(0, cells, TILE):
        part = slice(start, start + TILE)
        potential = lax.dot_general(
            screened[...], table[part, :], (((1,), (1,)), ((), ())), preferred_element_type=F32
        )
        potential = potential.reshape(rows_left, rows_right, TILE)
        left32, right32 = left[:, part].astype(F32), right[:, part].astype(F32)
        to_left[:, part] = (jnp.sum(potential * right32[None], axis=1) * factor).astype(BF16)
        to_right[:, part] = (jnp.sum(potential * left32[:, None], axis=0) * factor).astype(BF16)


def pair_fields(left, right, screening, slot, gmap):
    rows_left, cells = left.shape
    rows_right = right.shape[0]
    waves = gmap.shape[0]
    side = round(cells ** (1 / 3))
    vmem = pl.BlockSpec(memory_space=pltpu.VMEM)
    far = pl.BlockSpec(memory_space=pltpu.HBM)
    return pl.pallas_call(
        functools.partial(pair_kernel, side),
        out_shape=(
            jax.ShapeDtypeStruct((rows_left, cells), BF16),
            jax.ShapeDtypeStruct((rows_right, cells), BF16),
        ),
        in_specs=[pl.BlockSpec(memory_space=pltpu.SMEM), vmem, vmem, vmem, far],
        out_specs=(vmem, vmem),
        scratch_shapes=[
            pltpu.VMEM((waves, waves), BF16),
            pltpu.VMEM((side * side, waves), F32),
            pltpu.VMEM((side * side, waves), F32),
            pltpu.VMEM((cells, waves), BF16),
            pltpu.VMEM((rows_left * rows_right, cells), BF16),
            pltpu.VMEM((rows_left * rows_right, waves), BF16),
            pltpu.VMEM((rows_left * rows_right, waves), BF16),
            pltpu.SemaphoreType.DMA((3,)),
        ],
        compiler_params=pltpu.CompilerParams(vmem_limit_bytes=60 * 2**20),
    )(slot, gmap.reshape(1, waves), left, right, screening)


def fixed_shift(value, count, sign):
    shifts = (count - 1, count // 2)
    route = [
        (2 * i + core, 2 * ((i + sign * shift) % count) + core)
        for i in range(count)
        for core, shift in enumerate(shifts)
    ]
    return lax.ppermute(value, ("kq", "band"), route)


def shifted(value, shift, count):
    return lax.ppermute(value, "kq", [(i, (i + shift) % count) for i in range(count)])


def chosen_shift(value, steps, count, sign):
    moves = [lambda a, i=i: shifted(a, sign * i, count) for i in range(count)]
    return lax.switch(steps, moves, value)


def both_shifts(first, second, steps, count, sign):
    moves = [
        lambda a, b, i=i: (fixed_shift(a, count, sign), shifted(b, sign * i, count))
        for i in range(count)
    ]
    return lax.switch(steps, moves, first, second)


def cross(value):
    return lax.ppermute(value, "band", [(0, 1), (1, 0)])


def plan(pair_k, pair_q, core, count):
    last, half = count - 1, count // 2
    own = jnp.where(core == 0, last, half)
    other = last + half - own
    left, right = pair_k[: pair_q.shape[0], 0], pair_k[: pair_q.shape[0], 1]
    left_fixed, right_fixed = (left == last) | (left == half), (right == last) | (right == half)
    take_left = ((right == own) & (left != other)) | ~(left_fixed | right_fixed | (core != 0))
    take_right = ((left == own) & (right != other)) | ~(left_fixed | right_fixed | (core == 0))
    steps = jnp.sum(jnp.where(take_left, left, 0) + jnp.where(take_right, right, 0))
    together = jnp.sum((left_fixed & right_fixed).astype(jnp.int32))
    mine = ((left == last) | (right == last)) == (core == 0)
    slot = jnp.sum(jnp.where(mine, pair_q, 0))
    return steps, together, slot


def shards(orbitals, screening, pair_k, pair_q, gmap):
    count = lax.axis_size("kq")
    core = lax.axis_index("band")
    rows = orbitals.shape[1]
    first = core == 0
    steps, together, slot = plan(pair_k, pair_q, core, count)

    def lend(fixed, chosen):
        return jnp.where(first, fixed, chosen), cross(jnp.where(first, chosen, fixed))

    def regain(kept, lent):
        lent = cross(lent)
        return jnp.where(first, kept, lent), jnp.where(first, lent, kept)

    block = jnp.concatenate([orbitals[0], cross(orbitals[0])])
    block, steps, together, slot = lax.optimization_barrier((block, steps, together, slot))
    fixed, chosen = both_shifts(block, block, steps, count, -1)
    kept, given = lax.switch(together, [lambda a, b: (a, b), lend], fixed, chosen)
    kept, given = pair_fields(kept, given, screening, slot.reshape(1), gmap)
    fixed, chosen = lax.switch(together, [lambda a, b: (a, b), regain], kept, given)
    fixed = fixed_shift(fixed, count, 1)
    chosen = chosen_shift(chosen, steps, count, 1)
    total = fixed.astype(F32) + chosen.astype(F32)
    return (total[:rows] + cross(total[rows:].astype(BF16)).astype(F32))[None]


def solution(mesh):
    in_specs = (P("kq", "band", None), P("kq", None, None), P(), P("kq"), P())
    out_specs = P("kq", "band", None)
    return jax.shard_map(shards, mesh=mesh, in_specs=in_specs, out_specs=out_specs, check_vma=False)
```

```python
import functools
import math

import jax
import jax.numpy as jnp
from jax import lax
from jax.experimental import pallas as pl
from jax.experimental.pallas import tpu as pltpu
from jax.sharding import PartitionSpec as P

F32 = jnp.float32
BF16 = jnp.bfloat16
TILE = 256


def cosine(phase, side):
    phase = jnp.minimum(phase, side - phase)
    beyond = 4 * phase > side
    angle = jnp.where(beyond, side // 2 - phase, phase).astype(F32) * (2.0 * math.pi / side)
    square = angle * angle
    value = jnp.full(phase.shape, 1.0 / math.factorial(12), F32)
    for order in range(10, -1, -2):
        value = value * square + (-1.0) ** (order // 2) / math.factorial(order)
    return jnp.where(beyond, -value, value)


def circle(freq, side):
    steps = lax.broadcasted_iota(jnp.int32, (side, freq.shape[1]), 0)
    phase = lax.rem(steps * freq, side)
    return cosine(phase, side), cosine(lax.rem(phase + (side - side // 4), side), side)


def fill_table(gmap, table, plane, mirror, side, part):
    face, half = side * side, side // 2
    freq = gmap[:, part]
    cos_x, sin_x = circle(freq // face, side)
    cos_y, sin_y = circle(lax.rem(freq // side, side), side)
    cos_z, sin_z = circle(lax.rem(freq, side), side)
    cas_z, anti_z = cos_z + sin_z, cos_z - sin_z
    for y in range(side):
        rows = slice(y * side, (y + 1) * side)
        plane[rows, part] = cos_y[y : y + 1] * cas_z + sin_y[y : y + 1] * anti_z
        mirror[rows, part] = cos_y[y : y + 1] * anti_z - sin_y[y : y + 1] * cas_z
    turn = cos_x[half : half + 1].astype(BF16)
    along, against = plane[:, part], mirror[:, part]

    def put(x, value):
        value = value.astype(BF16)
        table[x * face : (x + 1) * face, part] = value
        other = (x + half) % side
        table[other * face : (other + 1) * face, part] = value * turn

    put(0, along)
    quarter = half // 2
    put(quarter, cos_x[quarter : quarter + 1] * along + sin_x[quarter : quarter + 1] * against)
    for x in range(1, quarter):
        even = cos_x[x : x + 1] * along
        odd = sin_x[x : x + 1] * against
        put(x, even + odd)
        put(side - x, even - odd)


def pair_kernel(
    side, slot, gmap, left, right, screening, to_left, to_right,
    matrix, plane, mirror, table, density, spectrum, screened, arrival,
):
    def fetch(i, source, target):
        copy = pltpu.make_async_copy(source, target, arrival.at[i])
        copy.start()
        return copy

    own = slot[0] - lax.axis_index("kq") * screening.shape[0]
    get_matrix = fetch(2, screening.at[own], matrix)

    rows_left, cells = left.shape
    rows_right = right.shape[0]
    waves = table.shape[1]
    factor = 1.0 / math.sqrt(cells)
    parts = [slice(start, start + TILE) for start in range(0, waves, TILE)]
    fill_table(gmap, table, plane, mirror, side, parts[0])
    for m in range(rows_left):
        density[m * rows_right : (m + 1) * rows_right, :] = left[m : m + 1, :] * right[...]
    for i, part in enumerate(parts):
        total = jnp.dot(density[...], table[:, part], preferred_element_type=F32)
        if i + 1 < len(parts):
            fill_table(gmap, table, plane, mirror, side, parts[i + 1])
        spectrum[:, part] = (total * factor).astype(BF16)
    get_matrix.wait()
    screened[...] = jnp.dot(
        spectrum[...], matrix[...], preferred_element_type=F32
    ).astype(BF16)
    for start in range(0, cells, TILE):
        part = slice(start, start + TILE)
        potential = lax.dot_general(
            screened[...], table[part, :], (((1,), (1,)), ((), ())), preferred_element_type=F32
        )
        potential = potential.reshape(rows_left, rows_right, TILE)
        left32, right32 = left[:, part].astype(F32), right[:, part].astype(F32)
        to_left[:, part] = (jnp.sum(potential * right32[None], axis=1) * factor).astype(BF16)
        to_right[:, part] = (jnp.sum(potential * left32[:, None], axis=0) * factor).astype(BF16)


def pair_fields(left, right, screening, slot, gmap):
    rows_left, cells = left.shape
    rows_right = right.shape[0]
    waves = gmap.shape[0]
    side = round(cells ** (1 / 3))
    vmem = pl.BlockSpec(memory_space=pltpu.VMEM)
    far = pl.BlockSpec(memory_space=pltpu.HBM)
    return pl.pallas_call(
        functools.partial(pair_kernel, side),
        out_shape=(
            jax.ShapeDtypeStruct((rows_left, cells), BF16),
            jax.ShapeDtypeStruct((rows_right, cells), BF16),
        ),
        in_specs=[pl.BlockSpec(memory_space=pltpu.SMEM), vmem, vmem, vmem, far],
        out_specs=(vmem, vmem),
        scratch_shapes=[
            pltpu.VMEM((waves, waves), BF16),
            pltpu.VMEM((side * side, waves), F32),
            pltpu.VMEM((side * side, waves), F32),
            pltpu.VMEM((cells, waves), BF16),
            pltpu.VMEM((rows_left * rows_right, cells), BF16),
            pltpu.VMEM((rows_left * rows_right, waves), BF16),
            pltpu.VMEM((rows_left * rows_right, waves), BF16),
            pltpu.SemaphoreType.DMA((3,)),
        ],
        compiler_params=pltpu.CompilerParams(vmem_limit_bytes=60 * 2**20),
    )(slot, gmap.reshape(1, waves), left, right, screening)


def fixed_shift(value, count, sign):
    shifts = (count - 1, count // 2)
    route = [
        (2 * i + core, 2 * ((i + sign * shift) % count) + core)
        for i in range(count)
        for core, shift in enumerate(shifts)
    ]
    return lax.ppermute(value, ("kq", "band"), route)


def shifted(value, shift, count):
    return lax.ppermute(value, "kq", [(i, (i + shift) % count) for i in range(count)])


def chosen_shift(value, steps, count, sign):
    moves = [lambda a, i=i: shifted(a, sign * i, count) for i in range(count)]
    return lax.switch(steps, moves, value)


def both_shifts(first, second, steps, count, sign):
    moves = [
        lambda a, b, i=i: (fixed_shift(a, count, sign), shifted(b, sign * i, count))
        for i in range(count)
    ]
    return lax.switch(steps, moves, first, second)


def cross(value):
    return lax.ppermute(value, "band", [(0, 1), (1, 0)])


def plan(pair_k, pair_q, core, count):
    last, half = count - 1, count // 2
    own = jnp.where(core == 0, last, half)
    other = last + half - own
    left, right = pair_k[: pair_q.shape[0], 0], pair_k[: pair_q.shape[0], 1]
    left_fixed, right_fixed = (left == last) | (left == half), (right == last) | (right == half)
    take_left = ((right == own) & (left != other)) | ~(left_fixed | right_fixed | (core != 0))
    take_right = ((left == own) & (right != other)) | ~(left_fixed | right_fixed | (core == 0))
    steps = jnp.sum(jnp.where(take_left, left, 0) + jnp.where(take_right, right, 0))
    together = jnp.sum((left_fixed & right_fixed).astype(jnp.int32))
    mine = ((left == last) | (right == last)) == (core == 0)
    slot = jnp.sum(jnp.where(mine, pair_q, 0))
    return steps, together, slot


def shards(orbitals, screening, pair_k, pair_q, gmap):
    count = lax.axis_size("kq")
    core = lax.axis_index("band")
    rows = orbitals.shape[1]
    first = core == 0
    steps, together, slot = plan(pair_k, pair_q, core, count)

    def lend(fixed, chosen):
        return jnp.where(first, fixed, chosen), cross(jnp.where(first, chosen, fixed))

    def regain(kept, lent):
        lent = cross(lent)
        return jnp.where(first, kept, lent), jnp.where(first, lent, kept)

    block = jnp.concatenate([orbitals[0], cross(orbitals[0])])
    block, steps, together, slot = lax.optimization_barrier((block, steps, together, slot))
    fixed, chosen = both_shifts(block, block, steps, count, -1)
    kept, given = lax.switch(together, [lambda a, b: (a, b), lend], fixed, chosen)
    kept, given = pair_fields(kept, given, screening, slot.reshape(1), gmap)
    fixed, chosen = lax.switch(together, [lambda a, b: (a, b), regain], kept, given)
    fixed = fixed_shift(fixed, count, 1)
    chosen = chosen_shift(chosen, steps, count, 1)
    total = fixed.astype(F32) + chosen.astype(F32)
    return (total[:rows] + cross(total[rows:].astype(BF16)).astype(F32))[None]


def solution(mesh):
    in_specs = (P("kq", "band", None), P("kq", None, None), P(), P("kq"), P())
    out_specs = P("kq", "band", None)
    return jax.shard_map(shards, mesh=mesh, in_specs=in_specs, out_specs=out_specs, check_vma=False)
```
